32 devices in a mesh: grp: 2 (over y), row: 4 (over z), col: 4 (over x, core).
Axes of the slice: x: 2, y: 2, z: 4, core: 2. Of those that a mesh axis runs over, the one named last changes fastest.
Arguments:
- out_first: float32 [512, 6144], P(('grp', 'col'), 'row'), parts along dimension 0, may hold values from -6 to 6
- out_second: float32 [512, 6144], P(('grp', 'col'), 'row'), parts along dimension 0, may hold values from -6 to 6
- grad_first: float32 [512, 6144], P(('grp', 'col'), 'row'), parts along dimension 0, may hold values from -6 to 6
- grad_second: float32 [512, 6144], P(('grp', 'col'), 'row'), parts along dimension 0, may hold values from -6 to 6
- w_query: bfloat16 [6144, 6144], P('row', 'col'), may hold values from -1 to 1
- w_key: bfloat16 [6144, 6144], P('row', 'col'), may hold values from -1 to 1
- w_value: bfloat16 [6144, 6144], P('row', 'col'), may hold values from -0.078125 to 0.078125
- w_out: bfloat16 [6144, 6144], P('col', 'row'), may hold values from -0.078125 to 0.078125
- w_up: bfloat16 [6144, 24576], P('row', 'col'), may hold values from -0.078125 to 0.078125
- w_down: bfloat16 [24576, 6144], P('col', 'row'), may hold values from -0.0390625 to 0.0390625
Outputs:
- input_first: float32 [512, 6144], P(('grp', 'col'), 'row'), parts along dimension 0
- input_second: float32 [512, 6144], P(('grp', 'col'), 'row'), parts along dimension 0
- grad_input_first: float32 [512, 6144], P(('grp', 'col'), 'row'), parts along dimension 0
- grad_input_second: float32 [512, 6144], P(('grp', 'col'), 'row'), parts along dimension 0
- grad_up: bfloat16 [12288, 24576], P(('grp', 'row'), 'col'), parts along dimension 0
- grad_down: bfloat16 [49152, 6144], P(('grp', 'col'), 'row'), parts along dimension 0
The draws below stay inside these ranges and needn't reach their ends.
There are 2 independent parts, one for each index of `grp`. The reference program is written for one: setup_inputs(seed, part) draws one part's arguments, and reference() takes and returns one part's arrays. A program takes and returns all parts, laid end to end along the dimension named above; an argument that names none is the same for every part. Nothing has to cross between parts.
All inputs are finite; a program needn't handle non-finite values.
Results may differ from the reference program's by a relative error of at most 0.04.
Values may be sent and summed in bfloat16 or wider, within the bound.
A program may use at most 256 MiB of HBM per device.

```python
import math
import jax
import jax.numpy as jnp
from jax import lax

D = 6144
FF = 24576
HEAD = 128
TOKENS = 256
N_ROW = 4


def draw_w_query(key, part):
    base = jax.random.normal(jax.random.fold_in(key, 1), (D, D), jnp.float32) / math.sqrt(D)
    return jnp.clip(base, -1.0, 1.0).astype(jnp.bfloat16)


def draw_w_key(key, part):
    base = jax.random.normal(jax.random.fold_in(key, 2), (D, D), jnp.float32) / math.sqrt(D)
    return jnp.clip(base, -1.0, 1.0).astype(jnp.bfloat16)


def block_scale(own_key, extent, split, least, top_value):
    loudness = 1.0
    for position, blocks in split:
        steps = jax.random.uniform(jax.random.fold_in(jax.random.fold_in(own_key, 6), position), (blocks,), jnp.float32, least / len(split), top_value / len(split))
        loudness = loudness * jnp.repeat(jnp.exp(steps), extent[position] // blocks).reshape((-1,) + (1,) * (len(extent) - 1 - position))
    return loudness


def gaussian(rng, extent, scale, most, split=(), kind=jnp.bfloat16):
    level = block_scale(rng, extent, split, -0.22, 0.18) if split else 1.0
    result = jax.random.normal(rng, extent, jnp.float32) * scale * level
    return jnp.minimum(jnp.maximum(result, -most), most).astype(kind)


def setup_inputs(seed: int = 0, part: int = 0) -> dict:
    splits = jax.random.split(jax.random.key(seed), 11)
    part_splits = jax.random.split(jax.random.fold_in(splits[10], part), 11)
    out_first = gaussian(part_splits[0], (TOKENS, D), 1.0, 6.0, ((0, 4), (1, 4)), jnp.float32)
    out_second = gaussian(part_splits[1], (TOKENS, D), 1.0, 6.0, ((0, 4), (1, 4)), jnp.float32)
    grad_first = gaussian(part_splits[2], (TOKENS, D), 1.0, 6.0, ((0, 4), (1, 4)), jnp.float32)
    grad_second = gaussian(part_splits[3], (TOKENS, D), 1.0, 6.0, ((0, 4), (1, 4)), jnp.float32)
    w_query = draw_w_query(jax.random.fold_in(splits[10], 71), part)
    w_key = draw_w_key(jax.random.fold_in(splits[10], 71), part)
    w_value = gaussian(splits[6], (D, D), D ** -0.5, 0.078125, ((0, 4), (1, 4)))
    w_out = gaussian(splits[7], (D, D), D ** -0.5, 0.078125, ((0, 4), (1, 4)))
    w_up = gaussian(splits[8], (D, FF), D ** -0.5, 0.078125, ((0, 4), (1, 4)))
    w_down = gaussian(splits[9], (FF, D), FF ** -0.5, 0.0390625, ((0, 4), (1, 4)))
    return dict(out_first=out_first, out_second=out_second, grad_first=grad_first, grad_second=grad_second, w_query=w_query, w_key=w_key, w_value=w_value, w_out=w_out, w_up=w_up, w_down=w_down)


def tanh_gelu(pre):
    inner = 0.7978845608028654 * (pre + 0.044715 * pre * pre * pre)
    slopes = jnp.tanh(inner)
    act_value = 0.5 * pre * (1.0 + slopes)
    change = 0.5 * (1.0 + slopes) + 0.5 * pre * (1.0 - slopes * slopes) * 0.7978845608028654 * (1.0 + 3.0 * 0.044715 * pre * pre)
    return (act_value, change)

def split_dot(first_op, second_op, parts):
    block_width = first_op.shape[1] // parts

    def add_block(running, block_index):
        start = (block_index * block_width).astype(jnp.int32)
        lhs_block = lax.dynamic_slice_in_dim(first_op, start, block_width, 1)
        rhs_block = lax.dynamic_slice_in_dim(second_op, start, block_width, 0)
        partial_value = jnp.dot(lhs_block, rhs_block, preferred_element_type=jnp.float32)
        rounded = lax.optimization_barrier(partial_value.astype(jnp.bfloat16))
        return (running + rounded.astype(jnp.float32), None)
    start_sum = jnp.zeros((first_op.shape[0], second_op.shape[1]), jnp.float32)
    running, unused = lax.scan(add_block, start_sum, jnp.arange(parts).astype(jnp.int32))
    return running

def block_sums(score_rows, token_rows, parts, factor):
    rows_block = token_rows.shape[0] // parts

    def add_block(running, block_index):
        start = (block_index * rows_block).astype(jnp.int32)
        lhs_block = lax.dynamic_slice_in_dim(score_rows, start, rows_block, 1).astype(jnp.float32)
        rhs_block = lax.dynamic_slice_in_dim(token_rows, start, rows_block, 0).astype(jnp.float32)
        partial_value = factor * jnp.einsum('hqk,qhd->khd', lhs_block, rhs_block)
        rounded = lax.optimization_barrier(partial_value.astype(jnp.bfloat16))
        return (running + rounded.astype(jnp.float32), None)
    start_sum = jnp.zeros((score_rows.shape[2], token_rows.shape[1], token_rows.shape[2]), jnp.float32)
    running, unused = lax.scan(add_block, start_sum, jnp.arange(parts).astype(jnp.int32))
    return running

def reference(out_first, out_second, grad_first, grad_second, w_query, w_key, w_value, w_out, w_up, w_down):
    heads = D // HEAD
    score_scale = 1.0 / math.sqrt(HEAD)
    first_b = out_first.astype(jnp.bfloat16)
    grad_b = grad_second.astype(jnp.bfloat16)
    pre = split_dot(first_b, w_up, N_ROW)
    back = split_dot(grad_b, w_down.T, N_ROW)
    act_value, change = tanh_gelu(pre)
    hidden = act_value.astype(jnp.bfloat16)
    slopes = (back * change).astype(jnp.bfloat16)
    grad_up = jnp.dot(first_b.T, slopes, preferred_element_type=jnp.float32).astype(jnp.bfloat16)
    grad_down = jnp.dot(hidden.T, grad_b, preferred_element_type=jnp.float32).astype(jnp.bfloat16)
    input_second = out_second - jnp.dot(hidden, w_down, preferred_element_type=jnp.float32)
    grad_input_first = grad_first + jnp.dot(slopes, w_up.T, preferred_element_type=jnp.float32)
    mid_b = input_second.astype(jnp.bfloat16)
    carry_b = grad_input_first.astype(jnp.bfloat16)
    queries = split_dot(mid_b, w_query, N_ROW).astype(jnp.bfloat16)
    keys = split_dot(mid_b, w_key, N_ROW).astype(jnp.bfloat16)
    values = split_dot(mid_b, w_value, N_ROW).astype(jnp.bfloat16)
    out_grad = split_dot(carry_b, w_out.T, N_ROW).astype(jnp.bfloat16)
    query_heads = queries.reshape(TOKENS, heads, HEAD)
    key_heads = keys.reshape(TOKENS, heads, HEAD)
    value_heads = values.reshape(TOKENS, heads, HEAD)
    grad_heads = out_grad.reshape(TOKENS, heads, HEAD)
    scores = jnp.einsum('qhd,khd->hqk', query_heads.astype(jnp.float32), key_heads.astype(jnp.float32)) * score_scale
    positions = jnp.arange(TOKENS)
    allowed = positions[None, :] <= positions[:, None]
    scores = jnp.where(allowed[None], scores, -1e+30)
    peak = lax.optimization_barrier(jnp.max(scores, axis=-1, keepdims=True))
    weights = jnp.exp(scores - peak)
    probs = weights / lax.optimization_barrier(jnp.sum(weights, axis=-1, keepdims=True))
    probs_b = probs.astype(jnp.bfloat16)
    attended = jnp.einsum('hqk,khd->qhd', probs_b.astype(jnp.float32), value_heads.astype(jnp.float32)).astype(jnp.bfloat16).reshape(TOKENS, D)
    dprob = jnp.einsum('qhd,khd->hqk', grad_heads.astype(jnp.float32), value_heads.astype(jnp.float32))
    delta = lax.optimization_barrier(jnp.sum(probs * dprob, axis=-1, keepdims=True))
    dscore = probs * (dprob - delta)
    dscore_b = dscore.astype(jnp.bfloat16)
    grad_queries = (score_scale * jnp.einsum('hqk,khd->qhd', dscore_b.astype(jnp.float32), key_heads.astype(jnp.float32))).astype(jnp.bfloat16).reshape(TOKENS, D)
    grad_keys = block_sums(dscore_b, query_heads, N_ROW, score_scale).astype(jnp.bfloat16).reshape(TOKENS, D)
    grad_values = block_sums(probs_b, grad_heads, N_ROW, 1.0).astype(jnp.bfloat16).reshape(TOKENS, D)
    input_first = out_first - jnp.dot(attended, w_out, preferred_element_type=jnp.float32)
    grad_mid = jnp.dot(grad_queries, w_query.T, preferred_element_type=jnp.float32)
    grad_mid = grad_mid + jnp.dot(grad_keys, w_key.T, preferred_element_type=jnp.float32)
    grad_mid = grad_mid + jnp.dot(grad_values, w_value.T, preferred_element_type=jnp.float32)
    grad_input_second = grad_second + grad_mid
    return (input_first, input_second, grad_input_first, grad_input_second, grad_up, grad_down)
```

```python
import functools
import math

import jax
import jax.numpy as jnp
from jax import lax
from jax.experimental import pallas as pl
from jax.experimental.pallas import tpu as pltpu
from jax.sharding import PartitionSpec as P

HEAD = 128


def for_sending(array):
    return jax.tree.map(lambda a: a.astype(jnp.bfloat16) if a.dtype == jnp.float32 else a, array)


def tanh_gelu(pre):
    inner = 0.7978845608028654 * (pre + 0.044715 * pre * pre * pre)
    slopes = jnp.tanh(inner)
    act_value = 0.5 * pre * (1.0 + slopes)
    change = 0.5 * (1.0 + slopes) + 0.5 * pre * (1.0 - slopes * slopes) * 0.7978845608028654 * (
        1.0 + 3.0 * 0.044715 * pre * pre
    )
    return (act_value, change)


def times_trans(first_op, second_op):
    return lax.dot_general(
        first_op, second_op, (((1,), (1,)), ((), ())), preferred_element_type=jnp.float32
    )


def trans_times(first_op, second_op):
    return lax.dot_general(
        first_op, second_op, (((0,), (0,)), ((), ())), preferred_element_type=jnp.float32
    )


def col_panels(arrays):
    return (
        lax.all_gather(arrays[0], "col", axis=0, tiled=True),
        lax.all_gather(arrays[1], "col", axis=0, tiled=True),
    )


def col_totals(arrays):
    return (
        lax.psum_scatter(
            arrays[0].astype(jnp.bfloat16), "col", scatter_dimension=0, tiled=True
        ).astype(jnp.float32),
        lax.psum_scatter(
            arrays[1].astype(jnp.bfloat16), "col", scatter_dimension=0, tiled=True
        ).astype(jnp.float32),
    )


def row_panels(arrays):
    return (
        lax.all_gather(arrays[0], "row", axis=0, tiled=True),
        lax.all_gather(arrays[1], "row", axis=0, tiled=True),
    )


def row_totals(arrays):
    return jax.tree.map(
        lambda part: part.astype(jnp.float32),
        lax.psum_scatter(for_sending(arrays), "row", scatter_dimension=0, tiled=True),
    )

def chain_kernel(n, count, chunks, ds_of, middle, *refs):
    ins, out = refs[:count], refs[count]
    right_buf, left_buf = refs[count + 1 : count + 3]
    sems = refs[count + 3 :]
    me = lax.axis_index("row")
    has_left, has_right = me > 0, me < n - 1

    def copy(buf, kind, k, b, target):
        rows, cols = ds_of(b, k)
        part = buf.at[:, rows, cols]
        return pltpu.make_async_remote_copy(
            src_ref=part,
            dst_ref=part,
            send_sem=sems[2 * kind].at[k * n + b],
            recv_sem=sems[2 * kind + 1].at[k * n + b],
            device_id={"row": target},
            device_id_type=pl.DeviceIdType.MESH,
        )

    def rs_right(k, b):
        return copy(right_buf, 0, k, b, me + 1)

    def rs_left(k, b):
        return copy(left_buf, 1, k, b, me - 1)

    def ag_right(k, b):
        return copy(out, 2, k, b, me + 1)

    def ag_left(k, b):
        return copy(out, 3, k, b, me - 1)

    barrier = pltpu.get_barrier_semaphore()

    @pl.when(has_left)
    def _():
        pl.semaphore_signal(
            barrier, inc=1, device_id={"row": me - 1}, device_id_type=pl.DeviceIdType.MESH
        )

    @pl.when(has_right)
    def _():
        pl.semaphore_signal(
            barrier, inc=1, device_id={"row": me + 1}, device_id_type=pl.DeviceIdType.MESH
        )

    pl.semaphore_wait(barrier, has_left.astype(jnp.int32) + has_right.astype(jnp.int32))

    def own_into(buf, k, b, add):
        rows, cols = ds_of(b, k)

        @pl.loop(0, rows.size // 16)
        def _(r):
            piece = pl.ds(pl.multiple_of(rows.start + r * 16, 16), 16)
            for s in range(count):
                val = ins[s][piece, cols]
                if add:
                    val = (val.astype(jnp.float32) + buf[s, piece, cols].astype(jnp.float32)).astype(
                        jnp.bfloat16
                    )
                buf[s, piece, cols] = val

    def hop(buf, make, k, b, has_source):
        @pl.when(has_source)
        def _():
            make(k, b).wait_recv()
            own_into(buf, k, b, True)

        @pl.when(jnp.logical_not(has_source))
        def _():
            own_into(buf, k, b, False)

        make(k, b).start()

    def zero(buf, k):
        rows, cols = ds_of(me, k)
        buf[:, rows, cols] = jnp.zeros((count, rows.size, cols.size), jnp.bfloat16)

    def reduce(k):
        for j in range(n):

            @pl.when(n - 1 - j > me)
            def _():
                hop(right_buf, rs_right, k, n - 1 - j, has_left)

            @pl.when(j < me)
            def _():
                hop(left_buf, rs_left, k, j, has_right)

        @pl.when(has_left)
        def _():
            rs_right(k, me).wait_recv()

        @pl.when(jnp.logical_not(has_left))
        def _():
            zero(right_buf, k)

        @pl.when(has_right)
        def _():
            rs_left(k, me).wait_recv()

        @pl.when(jnp.logical_not(has_right))
        def _():
            zero(left_buf, k)

        rows, cols = ds_of(me, k)
        middle(ins, right_buf, left_buf, out, rows, cols)

        @pl.when(has_right)
        def _():
            ag_right(k, me).start()

        @pl.when(has_left)
        def _():
            ag_left(k, me).start()

    def gather(k):
        for d in range(1, n):

            @pl.when(me - d >= 0)
            def _():
                ag_right(k, me - d).wait_recv()

                @pl.when(has_right)
                def _():
                    ag_right(k, me - d).start()

            @pl.when(me + d < n)
            def _():
                ag_left(k, me + d).wait_recv()

                @pl.when(has_left)
                def _():
                    ag_left(k, me + d).start()

    reduce(0)

    @pl.loop(1, chunks)
    def _(k):
        reduce(k)
        gather(k - 1)

    gather(chunks - 1)

    @pl.loop(0, chunks)
    def _(k):
        for b in range(n):

            @pl.when(b > me)
            def _():
                rs_right(k, b).wait_send()

            @pl.when(b < me)
            def _():
                rs_left(k, b).wait_send()

            @pl.when(jnp.logical_and(b <= me, has_right))
            def _():
                ag_right(k, b).wait_send()

            @pl.when(jnp.logical_and(b >= me, has_left))
            def _():
                ag_left(k, b).wait_send()


def chain_exchange(n, arrays, chunks, ds_of, middle, collective_id):
    count = len(arrays)
    tokens, width = arrays[0].shape
    full = (count, tokens, width)
    return pl.pallas_call(
        functools.partial(chain_kernel, n, count, chunks, ds_of, middle),
        out_shape=jax.ShapeDtypeStruct(full, jnp.bfloat16),
        in_specs=[pl.BlockSpec(memory_space=pltpu.VMEM)] * count,
        out_specs=pl.BlockSpec(memory_space=pltpu.VMEM),
        scratch_shapes=[pltpu.VMEM(full, jnp.bfloat16)] * 2
        + [pltpu.SemaphoreType.DMA((chunks * n,))] * 8,
        compiler_params=pltpu.CompilerParams(
            collective_id=collective_id,
            has_side_effects=True,
            vmem_limit_bytes=min(60 << 20, (4 * count + 1) * tokens * width * 2 + (12 << 20)),
        ),
    )(*arrays)


def ffn_middle(ins, right_buf, left_buf, out, rows, cols):
    @pl.loop(0, rows.size // 16)
    def _(r):
        piece = pl.ds(pl.multiple_of(rows.start + r * 16, 16), 16)
        pre_sum, back_sum = (
            ins[s][piece, cols].astype(jnp.float32)
            + right_buf[s, piece, cols].astype(jnp.float32)
            + left_buf[s, piece, cols].astype(jnp.float32)
            for s in range(2)
        )
        act_value, change = tanh_gelu(pre_sum)
        out[0, piece, cols] = act_value.astype(jnp.bfloat16)
        out[1, piece, cols] = (back_sum * change).astype(jnp.bfloat16)


def attention_middle(ins, right_buf, left_buf, out, rows, cols):
    queries, keys, values, out_grad = (
        (
            ins[s][rows, cols].astype(jnp.float32)
            + right_buf[s, rows, cols].astype(jnp.float32)
            + left_buf[s, rows, cols].astype(jnp.float32)
        ).astype(jnp.bfloat16)
        for s in range(4)
    )
    score_scale = 1.0 / math.sqrt(HEAD)
    tokens = queries.shape[0]
    scores = times_trans(queries, keys) * score_scale
    query_pos = lax.broadcasted_iota(jnp.int32, (tokens, tokens), 0)
    key_pos = lax.broadcasted_iota(jnp.int32, (tokens, tokens), 1)
    scores = jnp.where(key_pos <= query_pos, scores, -1e30)
    peak = jnp.max(scores, axis=-1, keepdims=True)
    weights = jnp.exp(scores - peak)
    probs = weights / jnp.sum(weights, axis=-1, keepdims=True)
    probs_b = probs.astype(jnp.bfloat16)
    out[0, rows, cols] = jnp.dot(probs_b, values, preferred_element_type=jnp.float32).astype(
        jnp.bfloat16
    )
    dprob = times_trans(out_grad, values)
    delta = jnp.sum(probs * dprob, axis=-1, keepdims=True)
    dscore_b = (probs * (dprob - delta)).astype(jnp.bfloat16)
    out[1, rows, cols] = (
        score_scale * jnp.dot(dscore_b, keys, preferred_element_type=jnp.float32)
    ).astype(jnp.bfloat16)
    out[2, rows, cols] = (score_scale * trans_times(dscore_b, queries)).astype(jnp.bfloat16)
    out[3, rows, cols] = trans_times(probs_b, out_grad).astype(jnp.bfloat16)


def token_blocks(token_rows, chunk_width):
    def ds_of(block, chunk):
        return (
            pl.ds(pl.multiple_of(block * token_rows, 16), token_rows),
            pl.ds(pl.multiple_of(chunk * chunk_width, 128), chunk_width),
        )

    return ds_of


def head_blocks(tokens, heads):
    def ds_of(block, chunk):
        return (
            pl.ds(0, tokens),
            pl.ds(pl.multiple_of((block * heads + chunk) * HEAD, HEAD), HEAD),
        )

    return ds_of


def attention_by_tokens(projections):
    score_scale = 1.0 / math.sqrt(HEAD)
    queries, key_rows, value_rows, out_grad = row_totals(projections)
    queries = queries.astype(jnp.bfloat16)
    out_grad = out_grad.astype(jnp.bfloat16)
    keys_all, values_all = row_panels(
        (key_rows.astype(jnp.bfloat16), value_rows.astype(jnp.bfloat16))
    )
    rows_here = queries.shape[0]
    head_cols = queries.shape[1]
    heads_here = head_cols // HEAD
    key_count = keys_all.shape[0]
    query_heads = queries.reshape(rows_here, heads_here, HEAD)
    grad_heads = out_grad.reshape(rows_here, heads_here, HEAD)
    key_heads = keys_all.reshape(key_count, heads_here, HEAD)
    value_heads = values_all.reshape(key_count, heads_here, HEAD)
    query_pos = lax.axis_index("row") * rows_here + lax.iota(jnp.int32, rows_here)
    key_pos = lax.iota(jnp.int32, key_count)
    allowed = key_pos[None, :] <= query_pos[:, None]
    scores = (
        jnp.einsum("qhd,khd->hqk", query_heads, key_heads, preferred_element_type=jnp.float32)
        * score_scale
    )
    scores = jnp.where(allowed[None], scores, -1e30)
    peak = jnp.max(scores, axis=-1, keepdims=True)
    weights = jnp.exp(scores - peak)
    probs = weights / jnp.sum(weights, axis=-1, keepdims=True)
    probs_b = probs.astype(jnp.bfloat16)
    attended = (
        jnp.einsum("hqk,khd->qhd", probs_b, value_heads, preferred_element_type=jnp.float32)
        .astype(jnp.bfloat16)
        .reshape(rows_here, head_cols)
    )
    dprob = jnp.einsum("qhd,khd->hqk", grad_heads, value_heads, preferred_element_type=jnp.float32)
    delta = jnp.sum(probs * dprob, axis=-1, keepdims=True)
    dscore_b = (probs * (dprob - delta)).astype(jnp.bfloat16)
    grad_queries = (
        (
            score_scale
            * jnp.einsum("hqk,khd->qhd", dscore_b, key_heads, preferred_element_type=jnp.float32)
        )
        .astype(jnp.bfloat16)
        .reshape(rows_here, head_cols)
    )
    key_term = (
        score_scale
        * jnp.einsum("hqk,qhd->khd", dscore_b, query_heads, preferred_element_type=jnp.float32)
    ).reshape(key_count, head_cols)
    value_term = jnp.einsum(
        "hqk,qhd->khd", probs_b, grad_heads, preferred_element_type=jnp.float32
    ).reshape(key_count, head_cols)
    key_sum, value_sum = (
        lax.psum(key_term.astype(jnp.bfloat16), "row").astype(jnp.float32),
        lax.psum(value_term.astype(jnp.bfloat16), "row").astype(jnp.float32),
    )
    attended_all, gradq_all = row_panels((attended, grad_queries))
    gradk_all = key_sum.astype(jnp.bfloat16)
    gradv_all = value_sum.astype(jnp.bfloat16)
    return attended_all, gradq_all, gradk_all, gradv_all


def shards(
    out_first, out_second, grad_first, grad_second, w_query, w_key, w_value, w_out, w_up, w_down
):
    inputs_all, grads_all = col_panels(
        (out_first.astype(jnp.bfloat16), grad_second.astype(jnp.bfloat16))
    )
    pre_term = jnp.dot(inputs_all, w_up, preferred_element_type=jnp.float32)
    back_term = times_trans(grads_all, w_down)
    n_row = lax.axis_size("row")
    pre_term, back_term = for_sending((pre_term, back_term))
    token_rows, hidden_width = pre_term.shape[0] // n_row, pre_term.shape[1]
    ffn_chunks = max(c for c in (1, 2, 4, 8) if hidden_width % (c * 128) == 0)
    hidden_slope = chain_exchange(
        n_row,
        (pre_term, back_term),
        ffn_chunks,
        token_blocks(token_rows, hidden_width // ffn_chunks),
        ffn_middle,
        1,
    )
    hidden_all, slope_all = hidden_slope[0], hidden_slope[1]
    grad_down = trans_times(hidden_all, grads_all).astype(jnp.bfloat16)
    grad_up = trans_times(inputs_all, slope_all).astype(jnp.bfloat16)
    ffn_out, ffn_back = col_totals(
        (
            jnp.dot(hidden_all, w_down, preferred_element_type=jnp.float32),
            times_trans(slope_all, w_up),
        )
    )
    input_second = out_second - ffn_out
    grad_input_first = grad_first + ffn_back
    mid_all, carry_all = col_panels(
        (input_second.astype(jnp.bfloat16), grad_input_first.astype(jnp.bfloat16))
    )
    projections = (
        jnp.dot(mid_all, w_query, preferred_element_type=jnp.float32),
        jnp.dot(mid_all, w_key, preferred_element_type=jnp.float32),
        jnp.dot(mid_all, w_value, preferred_element_type=jnp.float32),
        times_trans(carry_all, w_out),
    )
    heads_local = w_query.shape[1] // HEAD
    if heads_local % n_row == 0:
        share = heads_local // n_row
        results = chain_exchange(
            n_row,
            for_sending(projections),
            share,
            head_blocks(projections[0].shape[0], share),
            attention_middle,
            2,
        )
        attended_all, gradq_all, gradk_all, gradv_all = (results[s] for s in range(4))
    else:
        attended_all, gradq_all, gradk_all, gradv_all = attention_by_tokens(projections)
    grad_mid = (
        times_trans(gradq_all, w_query)
        + times_trans(gradk_all, w_key)
        + times_trans(gradv_all, w_value)
    )
    attn_out, back_mid = col_totals(
        (jnp.dot(attended_all, w_out, preferred_element_type=jnp.float32), grad_mid)
    )
    input_first = out_first - attn_out
    grad_input_second = grad_second + back_mid
    return (input_first, input_second, grad_input_first, grad_input_second, grad_up, grad_down)


def solution(mesh):
    in_specs = (
        P(("grp", "col"), "row"),
        P(("grp", "col"), "row"),
        P(("grp", "col"), "row"),
        P(("grp", "col"), "row"),
        P("row", "col"),
        P("row", "col"),
        P("row", "col"),
        P("col", "row"),
        P("row", "col"),
        P("col", "row"),
    )
    out_specs = (
        P(("grp", "col"), "row"),
        P(("grp", "col"), "row"),
        P(("grp", "col"), "row"),
        P(("grp", "col"), "row"),
        P(("grp", "row"), "col"),
        P(("grp", "col"), "row"),
    )
    return jax.shard_map(shards, mesh=mesh, in_specs=in_specs, out_specs=out_specs, check_vma=False)
```

```python
import functools
import math

import jax
import jax.numpy as jnp
from jax import lax
from jax.experimental import pallas as pl
from jax.experimental.pallas import tpu as pltpu
from jax.sharding import PartitionSpec as P

HEAD = 128


def for_sending(array):
    return jax.tree.map(lambda a: a.astype(jnp.bfloat16) if a.dtype == jnp.float32 else a, array)


def tanh_gelu(pre):
    inner = 0.7978845608028654 * (pre + 0.044715 * pre * pre * pre)
    slopes = jnp.tanh(inner)
    act_value = 0.5 * pre * (1.0 + slopes)
    change = 0.5 * (1.0 + slopes) + 0.5 * pre * (1.0 - slopes * slopes) * 0.7978845608028654 * (
        1.0 + 3.0 * 0.044715 * pre * pre
    )
    return (act_value, change)


def times_trans(first_op, second_op):
    return lax.dot_general(
        first_op, second_op, (((1,), (1,)), ((), ())), preferred_element_type=jnp.float32
    )


def trans_times(first_op, second_op):
    return lax.dot_general(
        first_op, second_op, (((0,), (0,)), ((), ())), preferred_element_type=jnp.float32
    )


def col_panels(arrays):
    return (
        lax.all_gather(arrays[0], "col", axis=0, tiled=True),
        lax.all_gather(arrays[1], "col", axis=0, tiled=True),
    )


def col_totals(arrays):
    return (
        lax.psum_scatter(
            arrays[0].astype(jnp.bfloat16), "col", scatter_dimension=0, tiled=True
        ).astype(jnp.float32),
        lax.psum_scatter(
            arrays[1].astype(jnp.bfloat16), "col", scatter_dimension=0, tiled=True
        ).astype(jnp.float32),
    )


def row_panels(arrays):
    return (
        lax.all_gather(arrays[0], "row", axis=0, tiled=True),
        lax.all_gather(arrays[1], "row", axis=0, tiled=True),
    )


def row_totals(arrays):
    return jax.tree.map(
        lambda part: part.astype(jnp.float32),
        lax.psum_scatter(for_sending(arrays), "row", scatter_dimension=0, tiled=True),
    )

def chain_kernel(n, count, chunks, ds_of, middle, *refs):
    ins, out = refs[:count], refs[count]
    right_buf, left_buf = refs[count + 1 : count + 3]
    sems = refs[count + 3 :]
    me = lax.axis_index("row")
    has_left, has_right = me > 0, me < n - 1

    def copy(buf, kind, k, b, target):
        rows, cols = ds_of(b, k)
        part = buf.at[:, rows, cols]
        return pltpu.make_async_remote_copy(
            src_ref=part,
            dst_ref=part,
            send_sem=sems[2 * kind].at[k * n + b],
            recv_sem=sems[2 * kind + 1].at[k * n + b],
            device_id={"row": target},
            device_id_type=pl.DeviceIdType.MESH,
        )

    def rs_right(k, b):
        return copy(right_buf, 0, k, b, me + 1)

    def rs_left(k, b):
        return copy(left_buf, 1, k, b, me - 1)

    def ag_right(k, b):
        return copy(out, 2, k, b, me + 1)

    def ag_left(k, b):
        return copy(out, 3, k, b, me - 1)

    barrier = pltpu.get_barrier_semaphore()

    @pl.when(has_left)
    def _():
        pl.semaphore_signal(
            barrier, inc=1, device_id={"row": me - 1}, device_id_type=pl.DeviceIdType.MESH
        )

    @pl.when(has_right)
    def _():
        pl.semaphore_signal(
            barrier, inc=1, device_id={"row": me + 1}, device_id_type=pl.DeviceIdType.MESH
        )

    pl.semaphore_wait(barrier, has_left.astype(jnp.int32) + has_right.astype(jnp.int32))

    def own_into(buf, k, b, add):
        rows, cols = ds_of(b, k)

        @pl.loop(0, rows.size // 16)
        def _(r):
            piece = pl.ds(pl.multiple_of(rows.start + r * 16, 16), 16)
            for s in range(count):
                val = ins[s][piece, cols]
                if add:
                    val = (val.astype(jnp.float32) + buf[s, piece, cols].astype(jnp.float32)).astype(
                        jnp.bfloat16
                    )
                buf[s, piece, cols] = val

    def hop(buf, make, k, b, has_source):
        @pl.when(has_source)
        def _():
            make(k, b).wait_recv()
            own_into(buf, k, b, True)

        @pl.when(jnp.logical_not(has_source))
        def _():
            own_into(buf, k, b, False)

        make(k, b).start()

    def zero(buf, k):
        rows, cols = ds_of(me, k)
        buf[:, rows, cols] = jnp.zeros((count, rows.size, cols.size), jnp.bfloat16)

    def hops_right(k):
        for b in range(n - 1, 0, -1):

            @pl.when(b > me)
            def _():
                hop(right_buf, rs_right, k, b, has_left)

    def hops_left(k):
        for b in range(n - 1):

            @pl.when(b < me)
            def _():
                hop(left_buf, rs_left, k, b, has_right)

    def finish(k):
        @pl.when(has_left)
        def _():
            rs_right(k, me).wait_recv()

        @pl.when(jnp.logical_not(has_left))
        def _():
            zero(right_buf, k)

        @pl.when(has_right)
        def _():
            rs_left(k, me).wait_recv()

        @pl.when(jnp.logical_not(has_right))
        def _():
            zero(left_buf, k)

        rows, cols = ds_of(me, k)
        middle(ins, right_buf, left_buf, out, rows, cols)

        @pl.when(has_right)
        def _():
            ag_right(k, me).start()

        @pl.when(has_left)
        def _():
            ag_left(k, me).start()

    def gather(k, d):
        @pl.when(me - d >= 0)
        def _():
            ag_right(k, me - d).wait_recv()

            @pl.when(has_right)
            def _():
                ag_right(k, me - d).start()

        @pl.when(me + d < n)
        def _():
            ag_left(k, me + d).wait_recv()

            @pl.when(has_left)
            def _():
                ag_left(k, me + d).start()

    def stage(work, k):
        @pl.when(jnp.logical_and(k >= 0, k < chunks))
        def _():
            work(k)

    @pl.loop(0, chunks + 2 * n - 1)
    def _(t):
        stage(hops_right, t - me)
        stage(hops_left, t - (n - 1 - me))
        stage(finish, t - n)
        for d in range(1, n):
            stage(functools.partial(gather, d=d), t - n - d)

    @pl.loop(0, chunks)
    def _(k):
        for b in range(n):

            @pl.when(b > me)
            def _():
                rs_right(k, b).wait_send()

            @pl.when(b < me)
            def _():
                rs_left(k, b).wait_send()

            @pl.when(jnp.logical_and(b <= me, has_right))
            def _():
                ag_right(k, b).wait_send()

            @pl.when(jnp.logical_and(b >= me, has_left))
            def _():
                ag_left(k, b).wait_send()


def chain_exchange(n, arrays, chunks, ds_of, middle, collective_id):
    count = len(arrays)
    tokens, width = arrays[0].shape
    full = (count, tokens, width)
    return pl.pallas_call(
        functools.partial(chain_kernel, n, count, chunks, ds_of, middle),
        out_shape=jax.ShapeDtypeStruct(full, jnp.bfloat16),
        in_specs=[pl.BlockSpec(memory_space=pltpu.VMEM)] * count,
        out_specs=pl.BlockSpec(memory_space=pltpu.VMEM),
        scratch_shapes=[pltpu.VMEM(full, jnp.bfloat16)] * 2
        + [pltpu.SemaphoreType.DMA((chunks * n,))] * 8,
        compiler_params=pltpu.CompilerParams(
            collective_id=collective_id,
            has_side_effects=True,
            vmem_limit_bytes=min(60 << 20, (4 * count + 1) * tokens * width * 2 + (12 << 20)),
        ),
    )(*arrays)


def grad_kernel(left_ref, right_ref, out_ref):
    out_ref[...] = jnp.dot(
        left_ref[...], right_ref[...], preferred_element_type=jnp.float32
    ).astype(jnp.bfloat16)


def grad_product(left_t, stacked, index):
    rows, tokens = left_t.shape
    width = stacked.shape[2]
    block = next(b for b in (512, 256, 128, width) if width % b == 0)
    return pl.pallas_call(
        grad_kernel,
        grid=(width // block,),
        out_shape=jax.ShapeDtypeStruct((rows, width), jnp.bfloat16),
        in_specs=[
            pl.BlockSpec((rows, tokens), lambda j: (0, 0)),
            pl.BlockSpec((None, tokens, block), lambda j: (index, 0, j)),
        ],
        out_specs=pl.BlockSpec((rows, block), lambda j: (0, j)),
        compiler_params=pltpu.CompilerParams(vmem_limit_bytes=24 << 20),
        cost_estimate=pl.CostEstimate(
            flops=2 * rows * tokens * width,
            bytes_accessed=2 * (rows * width + rows * tokens + tokens * width),
            transcendentals=0,
        ),
    )(left_t, stacked)


def ffn_middle(ins, right_buf, left_buf, out, rows, cols):
    @pl.loop(0, rows.size // 16)
    def _(r):
        piece = pl.ds(pl.multiple_of(rows.start + r * 16, 16), 16)
        pre_sum, back_sum = (
            ins[s][piece, cols].astype(jnp.float32)
            + right_buf[s, piece, cols].astype(jnp.float32)
            + left_buf[s, piece, cols].astype(jnp.float32)
            for s in range(2)
        )
        act_value, change = tanh_gelu(pre_sum)
        out[0, piece, cols] = act_value.astype(jnp.bfloat16)
        out[1, piece, cols] = (back_sum * change).astype(jnp.bfloat16)


def attention_middle(ins, right_buf, left_buf, out, rows, cols):
    queries, keys, values, out_grad = (
        (
            ins[s][rows, cols].astype(jnp.float32)
            + right_buf[s, rows, cols].astype(jnp.float32)
            + left_buf[s, rows, cols].astype(jnp.float32)
        ).astype(jnp.bfloat16)
        for s in range(4)
    )
    score_scale = 1.0 / math.sqrt(HEAD)
    tokens = queries.shape[0]
    scores = times_trans(queries, keys) * score_scale
    query_pos = lax.broadcasted_iota(jnp.int32, (tokens, tokens), 0)
    key_pos = lax.broadcasted_iota(jnp.int32, (tokens, tokens), 1)
    scores = jnp.where(key_pos <= query_pos, scores, -1e30)
    peak = jnp.max(scores, axis=-1, keepdims=True)
    weights = jnp.exp(scores - peak)
    probs = weights / jnp.sum(weights, axis=-1, keepdims=True)
    probs_b = probs.astype(jnp.bfloat16)
    out[0, rows, cols] = jnp.dot(probs_b, values, preferred_element_type=jnp.float32).astype(
        jnp.bfloat16
    )
    dprob = times_trans(out_grad, values)
    delta = jnp.sum(probs * dprob, axis=-1, keepdims=True)
    dscore_b = (probs * (dprob - delta)).astype(jnp.bfloat16)
    out[1, rows, cols] = (
        score_scale * jnp.dot(dscore_b, keys, preferred_element_type=jnp.float32)
    ).astype(jnp.bfloat16)
    out[2, rows, cols] = (score_scale * trans_times(dscore_b, queries)).astype(jnp.bfloat16)
    out[3, rows, cols] = trans_times(probs_b, out_grad).astype(jnp.bfloat16)


def token_blocks(token_rows, chunk_width):
    def ds_of(block, chunk):
        return (
            pl.ds(pl.multiple_of(block * token_rows, 16), token_rows),
            pl.ds(pl.multiple_of(chunk * chunk_width, 128), chunk_width),
        )

    return ds_of


def head_blocks(tokens, heads):
    def ds_of(block, chunk):
        return (
            pl.ds(0, tokens),
            pl.ds(pl.multiple_of((block * heads + chunk) * HEAD, HEAD), HEAD),
        )

    return ds_of


def attention_by_tokens(projections):
    score_scale = 1.0 / math.sqrt(HEAD)
    queries, key_rows, value_rows, out_grad = row_totals(projections)
    queries = queries.astype(jnp.bfloat16)
    out_grad = out_grad.astype(jnp.bfloat16)
    keys_all, values_all = row_panels(
        (key_rows.astype(jnp.bfloat16), value_rows.astype(jnp.bfloat16))
    )
    rows_here = queries.shape[0]
    head_cols = queries.shape[1]
    heads_here = head_cols // HEAD
    key_count = keys_all.shape[0]
    query_heads = queries.reshape(rows_here, heads_here, HEAD)
    grad_heads = out_grad.reshape(rows_here, heads_here, HEAD)
    key_heads = keys_all.reshape(key_count, heads_here, HEAD)
    value_heads = values_all.reshape(key_count, heads_here, HEAD)
    query_pos = lax.axis_index("row") * rows_here + lax.iota(jnp.int32, rows_here)
    key_pos = lax.iota(jnp.int32, key_count)
    allowed = key_pos[None, :] <= query_pos[:, None]
    scores = (
        jnp.einsum("qhd,khd->hqk", query_heads, key_heads, preferred_element_type=jnp.float32)
        * score_scale
    )
    scores = jnp.where(allowed[None], scores, -1e30)
    peak = jnp.max(scores, axis=-1, keepdims=True)
    weights = jnp.exp(scores - peak)
    probs = weights / jnp.sum(weights, axis=-1, keepdims=True)
    probs_b = probs.astype(jnp.bfloat16)
    attended = (
        jnp.einsum("hqk,khd->qhd", probs_b, value_heads, preferred_element_type=jnp.float32)
        .astype(jnp.bfloat16)
        .reshape(rows_here, head_cols)
    )
    dprob = jnp.einsum("qhd,khd->hqk", grad_heads, value_heads, preferred_element_type=jnp.float32)
    delta = jnp.sum(probs * dprob, axis=-1, keepdims=True)
    dscore_b = (probs * (dprob - delta)).astype(jnp.bfloat16)
    grad_queries = (
        (
            score_scale
            * jnp.einsum("hqk,khd->qhd", dscore_b, key_heads, preferred_element_type=jnp.float32)
        )
        .astype(jnp.bfloat16)
        .reshape(rows_here, head_cols)
    )
    key_term = (
        score_scale
        * jnp.einsum("hqk,qhd->khd", dscore_b, query_heads, preferred_element_type=jnp.float32)
    ).reshape(key_count, head_cols)
    value_term = jnp.einsum(
        "hqk,qhd->khd", probs_b, grad_heads, preferred_element_type=jnp.float32
    ).reshape(key_count, head_cols)
    key_sum, value_sum = (
        lax.psum(key_term.astype(jnp.bfloat16), "row").astype(jnp.float32),
        lax.psum(value_term.astype(jnp.bfloat16), "row").astype(jnp.float32),
    )
    attended_all, gradq_all = row_panels((attended, grad_queries))
    gradk_all = key_sum.astype(jnp.bfloat16)
    gradv_all = value_sum.astype(jnp.bfloat16)
    return attended_all, gradq_all, gradk_all, gradv_all


def shards(
    out_first, out_second, grad_first, grad_second, w_query, w_key, w_value, w_out, w_up, w_down
):
    inputs_all, grads_all = col_panels(
        (out_first.astype(jnp.bfloat16), grad_second.astype(jnp.bfloat16))
    )
    pre_term = jnp.dot(inputs_all, w_up, preferred_element_type=jnp.float32)
    back_term = times_trans(grads_all, w_down)
    n_row = lax.axis_size("row")
    pre_term, back_term = for_sending((pre_term, back_term))
    token_rows, hidden_width = pre_term.shape[0] // n_row, pre_term.shape[1]
    ffn_chunks = max(c for c in (1, 2, 4, 8, 16) if hidden_width % (c * 128) == 0)
    hidden_slope = chain_exchange(
        n_row,
        (pre_term, back_term),
        ffn_chunks,
        token_blocks(token_rows, hidden_width // ffn_chunks),
        ffn_middle,
        1,
    )
    hidden_all, slope_all = hidden_slope[0], hidden_slope[1]
    grad_down = trans_times(hidden_all, grads_all).astype(jnp.bfloat16)
    grad_up = grad_product(inputs_all.T, hidden_slope, 1)
    ffn_out, ffn_back = col_totals(
        (
            jnp.dot(hidden_all, w_down, preferred_element_type=jnp.float32),
            times_trans(slope_all, w_up),
        )
    )
    input_second = out_second - ffn_out
    grad_input_first = grad_first + ffn_back
    mid_all, carry_all = col_panels(
        (input_second.astype(jnp.bfloat16), grad_input_first.astype(jnp.bfloat16))
    )
    projections = (
        jnp.dot(mid_all, w_query, preferred_element_type=jnp.float32),
        jnp.dot(mid_all, w_key, preferred_element_type=jnp.float32),
        jnp.dot(mid_all, w_value, preferred_element_type=jnp.float32),
        times_trans(carry_all, w_out),
    )
    heads_local = w_query.shape[1] // HEAD
    if heads_local % n_row == 0:
        share = heads_local // n_row
        results = chain_exchange(
            n_row,
            for_sending(projections),
            share,
            head_blocks(projections[0].shape[0], share),
            attention_middle,
            2,
        )
        attended_all, gradq_all, gradk_all, gradv_all = (results[s] for s in range(4))
    else:
        attended_all, gradq_all, gradk_all, gradv_all = attention_by_tokens(projections)
    grad_mid = (
        times_trans(gradq_all, w_query)
        + times_trans(gradk_all, w_key)
        + times_trans(gradv_all, w_value)
    )
    attn_out, back_mid = col_totals(
        (jnp.dot(attended_all, w_out, preferred_element_type=jnp.float32), grad_mid)
    )
    input_first = out_first - attn_out
    grad_input_second = grad_second + back_mid
    return (input_first, input_second, grad_input_first, grad_input_second, grad_up, grad_down)


def solution(mesh):
    in_specs = (
        P(("grp", "col"), "row"),
        P(("grp", "col"), "row"),
        P(("grp", "col"), "row"),
        P(("grp", "col"), "row"),
        P("row", "col"),
        P("row", "col"),
        P("row", "col"),
        P("col", "row"),
        P("row", "col"),
        P("col", "row"),
    )
    out_specs = (
        P(("grp", "col"), "row"),
        P(("grp", "col"), "row"),
        P(("grp", "col"), "row"),
        P(("grp", "col"), "row"),
        P(("grp", "row"), "col"),
        P(("grp", "col"), "row"),
    )
    return jax.shard_map(shards, mesh=mesh, in_specs=in_specs, out_specs=out_specs, check_vma=False)
```
